256 devices in a mesh: stn: 128 (over x, y_hi, z, core), blk: 2 (over y_lo).
Axes of the slice: x: 4, y: 4 (y_hi: 2, y_lo: 2; y = y_hi * 2 + y_lo), z: 8, core: 2. Of those that a mesh axis runs over, the one named last changes fastest.
Arguments:
- voltages: bfloat16 [1024, 2, 63, 2, 4096], P('stn', 'blk'), may hold values from -6 to 6
- station_map: int32 [512], replicated, may hold values from 0 to 511, each once
- chan_counts: int32 [128], replicated, may hold values from 1 to 3, 256 in all
Outputs:
- visibilities: bfloat16 [128, 3, 2, 1024, 1024], P('stn', None, None, 'blk')
The draws below stay inside these ranges and needn't reach their ends.
Inputs may be any that keep to these rules, and one draw needn't show every extreme that they name: A permutation: stream rows 2 q and 2 q + 1 of voltages are the two polarizations of station station_map[q]. `chan_counts`: the counts sum to 256; the largest is 3; device d of stn correlates the consecutive channels that start at the sum of the counts before it.
All inputs are finite; a program needn't handle non-finite values.
Results may differ from the reference program's by a relative error of at most 0.0056.
Values may be sent and summed in bfloat16 or wider, within the bound.
A program may use at most 192 MiB of HBM per device.

```python
import math
import jax
import jax.numpy as jnp
import numpy as np
from jax import lax

STATIONS = 512
FFT_LEN = 4096
TAPS = 16
CAP = 3
NSPEC = 48
FRAMES = 63
BAND = 256
N_STN = 128
N_BLK = 2


def level_of(stream_key, dims, pieces, smallest, high):
    gain, own = 1.0, jax.random.fold_in(stream_key, 6)
    for dim, blocks in pieces:
        draws = jnp.exp(jax.random.uniform(jax.random.fold_in(own, dim), (blocks,), jnp.float32, smallest / len(pieces), high / len(pieces)))
        gain = gain * jnp.repeat(draws, dims[dim] // blocks).reshape([-1 if axis == dim else 1 for axis in range(len(dims))])
    return gain


def split_up(amount, total, reach, skew):
    weights = [(1 << 20) // math.isqrt(rank ** skew) + 1 for rank in range(2, amount + 1)]
    spare, holding = total - reach - (amount - 1), [1] * (amount - 1)
    while spare > 0:
        movable = [i for i in range(amount - 1) if holding[i] < reach]
        whole, left = sum([weights[i] for i in movable]), spare
        for i in movable:
            addition = min(reach - holding[i], max(1, left * weights[i] // whole), spare)
            holding[i] = holding[i] + addition
            spare = spare - addition
    return np.array([reach] + holding)


def uneven(stream_key, count, total, reach, lean):
    if count == 2:
        one = jax.random.randint(stream_key, (), max(1, total - reach), min(reach, total - 1) + 1)
        return jnp.stack([one, total - one])
    sizes = jnp.asarray(split_up(count, total, reach, lean), jnp.int32)
    pairs = (count - 1) // 2
    source_of, sink = sizes[1:1 + 2 * pairs:2], sizes[2:2 + 2 * pairs:2]
    room = jnp.minimum(source_of - 1, reach - sink)
    passed = jax.random.randint(jax.random.fold_in(stream_key, 1), (pairs,), 0, 1 << 20) % (room + 1)
    sizes = sizes.at[1:1 + 2 * pairs:2].set(source_of - passed).at[2:2 + 2 * pairs:2].set(sink + passed)
    return sizes[jax.random.permutation(jax.random.fold_in(stream_key, 2), count)]


def centred(own_key, extent, scale, limit, shards=(), kind=jnp.bfloat16):
    loudness = level_of(own_key, extent, shards, -0.22, 0.18) if shards else 1.0
    drawn = jax.random.normal(own_key, extent, jnp.float32) * scale * loudness
    return jnp.minimum(jnp.maximum(drawn, -limit), limit).astype(kind)


def setup_inputs(seed: int = 0) -> dict:
    splits = jax.random.split(jax.random.key(seed), 4)
    voltages = centred(splits[0], (2 * STATIONS, N_BLK, FRAMES, 2, FFT_LEN), 1.0, 6.0, ((0, 128), (1, 2)))
    station_map = jax.random.permutation(splits[1], STATIONS).astype(jnp.int32)
    chan_counts = uneven(splits[2], N_STN, BAND, CAP, 0).astype(jnp.int32)
    return dict(voltages=voltages, station_map=station_map, chan_counts=chan_counts)


def prototype(tap_count, frame_len):
    span_len = tap_count * frame_len
    points = jnp.arange(span_len, dtype=jnp.float32) + 0.5
    window = 0.5 - 0.5 * jnp.cos(2.0 * math.pi * points / span_len)
    shifted = math.pi * (points - span_len / 2.0) / frame_len
    filt_vals = jnp.sin(shifted) / shifted * window
    filt_vals = filt_vals / jnp.sqrt(jnp.sum(filt_vals * filt_vals))
    return filt_vals.reshape(tap_count, frame_len)

def reference(voltages, station_map, chan_counts):
    row_count = 2 * STATIONS
    band_len = BAND
    taper_table = prototype(TAPS, FFT_LEN)
    block_rows = math.gcd(row_count, 64)

    def channelize(volt_block):
        folded = jnp.zeros((block_rows, N_BLK, NSPEC, 2, FFT_LEN), jnp.float32)
        for tap_idx in range(TAPS):
            folded = folded + volt_block[:, :, tap_idx:tap_idx + NSPEC].astype(jnp.float32) * taper_table[tap_idx]
        signal = lax.complex(folded[:, :, :, 0], folded[:, :, :, 1])
        spectrum = jnp.fft.fft(signal, axis=-1)[..., :band_len]
        return jnp.stack([jnp.real(spectrum), jnp.imag(spectrum)], axis=3).astype(jnp.bfloat16)
    shaped = voltages.reshape(row_count // block_rows, block_rows, N_BLK, FRAMES, 2, FFT_LEN)
    spectra = lax.map(channelize, shaped)
    spectra = spectra.reshape(row_count, N_BLK * NSPEC, 2, band_len)
    inverse = jnp.zeros((STATIONS,), jnp.int32).at[station_map].set(jnp.arange(STATIONS, dtype=jnp.int32))
    true_rows = (2 * inverse[:, None] + jnp.arange(2, dtype=jnp.int32)[None, :]).reshape(-1)
    spectra = spectra[true_rows]
    offsets = jnp.cumsum(chan_counts) - chan_counts
    samples = N_BLK * NSPEC

    def correlate(slot_idx):
        device = slot_idx // CAP
        within = slot_idx % CAP
        live_count = chan_counts[device]
        channel = offsets[device] + jnp.minimum(within, live_count - 1)
        picked = lax.dynamic_index_in_dim(spectra, channel, axis=3, keepdims=False)
        real_part = picked[:, :, 0]
        imag_part = picked[:, :, 1]
        joined = jnp.concatenate([real_part, imag_part], axis=1)
        turned = jnp.concatenate([imag_part, -real_part], axis=1)
        vis_real = jnp.dot(joined, joined.T, preferred_element_type=jnp.float32)
        vis_imag = jnp.dot(turned, joined.T, preferred_element_type=jnp.float32)
        valid_mask = (within < live_count).astype(jnp.float32)
        return (jnp.stack([vis_real, vis_imag]) * (valid_mask / samples)).astype(jnp.bfloat16)
    slot_ids = jnp.arange(N_STN * CAP, dtype=jnp.int32)
    result = lax.map(correlate, slot_ids)
    return result.reshape(N_STN, CAP, 2, row_count, row_count)
```

```python
import functools
import math

import jax
import jax.numpy as jnp
import ml_dtypes
import numpy as np
from jax import lax
from jax.experimental import pallas as pl
from jax.experimental.pallas import tpu as pltpu
from jax.sharding import PartitionSpec as P

FFT_LEN = 4096
TAPS = 16
CAP = 3
NSPEC = 48
FRAMES = 63
STREAMS = 8
BAND = 256
LANES = 128
TILES = FFT_LEN // LANES
STEP_TILES = 2
STEPS = TILES // STEP_TILES
ROWS = NSPEC * STREAMS * 2
SLOTS = 4
CENTRE = (TAPS // 2 - 1, TAPS // 2)
OUTER = sorted((t for t in range(TAPS) if t not in CENTRE), key=lambda t: -abs(t - 7.5))
MESH = pl.DeviceIdType.MESH


def taper_tiles():
    points = np.arange(TAPS * FFT_LEN) + 0.5
    span_len = TAPS * FFT_LEN
    filt = np.sinc((points - span_len / 2) / FFT_LEN) * (
        0.5 - 0.5 * np.cos(2.0 * math.pi * points / span_len)
    )
    filt = filt / np.sqrt(np.sum(filt * filt))
    tiles = filt.reshape(TAPS, TILES, LANES).transpose(1, 0, 2)
    return np.ascontiguousarray(tiles.astype(np.float32))


def dft_table():
    positions = np.arange(FFT_LEN)
    channels = np.arange(BAND)
    phase = (positions[:, None] * channels[None, :] % FFT_LEN) * (2.0 * math.pi / FFT_LEN)
    table = np.concatenate([np.cos(phase), np.sin(phase)], axis=1)
    return table.astype(ml_dtypes.bfloat16)


def fold_step(tap_ref, frames, step, lhs):
    for kk in range(STEP_TILES):
        taps = tap_ref[step * STEP_TILES + kk]
        wide = [jnp.broadcast_to(taps[t : t + 1], (16, LANES)) for t in range(TAPS)]
        low = {t: wide[t].astype(jnp.bfloat16) for t in OUTER}
        volts = [frames[r, kk] for r in range(FRAMES)]
        full = {r: volts[r].astype(jnp.float32) for r in range(CENTRE[0], NSPEC + CENTRE[1])}
        for s in range(NSPEC):
            small = low[OUTER[0]] * volts[s + OUTER[0]]
            for t in OUTER[1:]:
                small = small + low[t] * volts[s + t]
            total = small.astype(jnp.float32)
            for t in CENTRE:
                total = total + wide[t] * full[s + t]
            lhs[s * 16 : (s + 1) * 16, kk * LANES : (kk + 1) * LANES] = total.astype(jnp.bfloat16)


def channelize(volt_ref, tap_ref, table_ref, count_ref, out_ref, frames, tables, lhs_a, lhs_b, acc, spec, wide, sems, table_sems):
    def copies(step):
        slot = lax.rem(step, SLOTS)
        tile = step * STEP_TILES
        made = []
        for a in range(STREAMS):
            made.append(
                pltpu.make_async_copy(
                    volt_ref.at[a, :, pl.ds(tile, STEP_TILES)],
                    frames.at[slot, :, :, a],
                    sems.at[slot, a],
                )
            )
        made.append(
            pltpu.make_async_copy(
                table_ref.at[pl.ds(tile * LANES, STEP_TILES * LANES)],
                tables.at[slot],
                table_sems.at[slot],
            )
        )
        return made

    def start(step):
        for copy in copies(step):
            copy.start()

    def wait(step):
        for copy in copies(step):
            copy.wait()

    view = frames.reshape(SLOTS, FRAMES, STEP_TILES, 16, LANES)

    def fold(step, lhs):
        fold_step(tap_ref, view.at[lax.rem(step, SLOTS)], step, lhs)

    def multiply(step, lhs):
        got = jnp.dot(
            lhs[...], tables[lax.rem(step, SLOTS)], preferred_element_type=jnp.float32
        )
        for q in range(4):
            acc[q] += got[:, q * LANES : (q + 1) * LANES]

    for step in range(3):
        start(step)
    acc[...] = jnp.zeros_like(acc)
    wait(0)
    fold(0, lhs_a)

    def pair(j, carry):
        step = 2 * j
        wait(step + 1)
        start(step + 3)
        fold(step + 1, lhs_b)
        multiply(step, lhs_a)
        wait(step + 2)

        @pl.when(step + 4 < STEPS)
        def _():
            start(step + 4)

        fold(step + 2, lhs_a)
        multiply(step + 1, lhs_b)
        return carry

    lax.fori_loop(0, STEPS // 2 - 1, pair, 0)
    wait(STEPS - 1)
    fold(STEPS - 1, lhs_b)
    multiply(STEPS - 2, lhs_a)
    multiply(STEPS - 1, lhs_b)

    for a in range(STREAMS):
        part = {}
        for p in range(2):
            for q in range(4):
                part[p, q] = acc[q, pl.ds(2 * a + p, NSPEC, stride=16), :]
        for q in range(2):
            cols = slice(q * LANES, (q + 1) * LANES)
            rows = slice(a * NSPEC, (a + 1) * NSPEC)
            spec[0, rows, cols] = (part[0, q] + part[1, q + 2]).astype(jnp.bfloat16)
            spec[1, rows, cols] = (part[1, q] - part[0, q + 2]).astype(jnp.bfloat16)

    row = lax.broadcasted_iota(jnp.int32, (LANES, LANES), 0)
    device = (row & 7) * 16 + (row >> 3)
    lane = lax.broadcasted_iota(jnp.int32, (LANES, LANES), 1)
    counts = jnp.broadcast_to(count_ref[...], (LANES, LANES)).astype(jnp.float32)
    offset = jnp.sum(jnp.where(lane < device, counts, 0.0), axis=1, keepdims=True)
    count = jnp.sum(jnp.where(lane == device, counts, 0.0), axis=1, keepdims=True)
    band = lax.broadcasted_iota(jnp.int32, (LANES, BAND), 1)
    flat = out_ref.reshape(CAP, LANES * 6, LANES)
    for c in range(CAP):
        pick = (offset + jnp.minimum(float(c), count - 1.0)).astype(jnp.int32)
        chosen = jnp.where(band == pick, 1.0, 0.0).astype(jnp.bfloat16)
        for p in range(2):
            turned = lax.dot_general(
                chosen, spec[p], (((1,), (1,)), ((), ())), preferred_element_type=jnp.float32
            )
            for q in range(3):
                wide[pl.ds(2 * q + p, LANES, stride=6), :] = turned[:, q * LANES : (q + 1) * LANES]
        flat[c] = wide[...].astype(jnp.bfloat16)


def run_channelize(voltages, chan_counts):
    tiles = voltages.reshape(STREAMS, FRAMES, 2, TILES, LANES).transpose(0, 1, 3, 2, 4)
    vmem = pl.BlockSpec(memory_space=pltpu.VMEM)
    hbm = pl.BlockSpec(memory_space=pl.ANY)
    return pl.pallas_call(
        channelize,
        out_shape=jax.ShapeDtypeStruct((CAP, 16, 8, 3, 2, LANES), jnp.bfloat16),
        in_specs=[hbm, vmem, hbm, vmem],
        out_specs=vmem,
        scratch_shapes=[
            pltpu.VMEM((SLOTS, FRAMES, STEP_TILES, STREAMS, 2, LANES), jnp.bfloat16),
            pltpu.VMEM((SLOTS, STEP_TILES * LANES, 2 * BAND), jnp.bfloat16),
            pltpu.VMEM((ROWS, STEP_TILES * LANES), jnp.bfloat16),
            pltpu.VMEM((ROWS, STEP_TILES * LANES), jnp.bfloat16),
            pltpu.VMEM((4, ROWS, LANES), jnp.float32),
            pltpu.VMEM((2, ROWS // 2, BAND), jnp.bfloat16),
            pltpu.VMEM((LANES * 6, LANES), jnp.float32),
            pltpu.SemaphoreType.DMA((SLOTS, STREAMS)),
            pltpu.SemaphoreType.DMA((SLOTS,)),
        ],
        compiler_params=pltpu.CompilerParams(vmem_limit_bytes=60 * 1024 * 1024),
        name="channelize",
    )(tiles, jnp.asarray(taper_tiles()), jnp.asarray(dft_table()), chan_counts.reshape(1, LANES))


def corner_turn(sent, got, stage, other, send_z, recv_z, send_x, recv_x, send_y, recv_y, local_sems):
    stn = lax.axis_index("stn")
    blk = lax.axis_index("blk")
    g = lax.rem(stn, 16)
    h = lax.div(stn, 16)
    x = lax.div(h, 2)
    y_hi = lax.rem(h, 2)
    y = 2 * y_hi + blk

    def at(x_to, y_hi_to, g_to):
        return (x_to * 2 + y_hi_to) * 16 + g_to

    near = {"stn": stn, "blk": 1 - blk}
    cross = {"stn": at(x, 1 - y_hi, g), "blk": 1 - blk}
    ring_z = [{"stn": at(x, y_hi, lax.rem(g + j, 16)), "blk": blk} for j in range(1, 16)]
    ring_x = [{"stn": at(lax.rem(x + j, 4), y_hi, g), "blk": blk} for j in range(1, 4)]

    barrier = pltpu.get_barrier_semaphore()
    partners = [*ring_z, *ring_x, near, cross]
    for partner in partners:
        pl.semaphore_signal(barrier, inc=1, device_id=partner, device_id_type=MESH)
    pl.semaphore_wait(barrier, len(partners))

    def remote(src, dst, send, recv, device):
        copy = pltpu.make_async_remote_copy(
            src_ref=src, dst_ref=dst, send_sem=send, recv_sem=recv, device_id=device, device_id_type=MESH
        )
        copy.start()

    def drain(ref, sem):
        pltpu.make_async_copy(ref, ref, sem).wait()

    def own_z(c):
        return pltpu.make_async_copy(sent.at[c, g], stage.at[c, g], local_sems.at[0, c])

    def own_x(c, half):
        if half == 0:
            return pltpu.make_async_copy(
                stage.at[c, :, x * 2 + y_hi], got.at[c, y, x], local_sems.at[1, c]
            )
        return pltpu.make_async_copy(
            stage.at[c, :, x * 2 + 1 - y_hi], other.at[c, x], local_sems.at[2, c]
        )

    def go_z(c):
        own_z(c).start()
        for j in range(1, 16):
            remote(
                sent.at[c, lax.rem(g + j, 16)], stage.at[c, g], send_z.at[c], recv_z.at[c], ring_z[j - 1]
            )

    def go_x(c):
        own_z(c).wait()
        drain(stage.at[c, pl.ds(0, 15)], recv_z.at[c])
        own_x(c, 0).start()
        own_x(c, 1).start()
        for j in range(1, 4):
            x_to = lax.rem(x + j, 4)
            remote(
                stage.at[c, :, x_to * 2 + 1 - y_hi], other.at[c, x], send_x.at[1, c], recv_x.at[1, c], ring_x[j - 1]
            )
        for j in range(1, 4):
            x_to = lax.rem(x + j, 4)
            remote(
                stage.at[c, :, x_to * 2 + y_hi], got.at[c, y, x], send_x.at[0, c], recv_x.at[0, c], ring_x[j - 1]
            )

    def go_y(c):
        own_x(c, 1).wait()
        drain(other.at[c, pl.ds(0, 3)], recv_x.at[1, c])
        remote(other.at[c], got.at[c, y], send_y.at[0, c], recv_y.at[0, c], cross)
        own_x(c, 0).wait()
        drain(other.at[c, pl.ds(0, 3)], recv_x.at[0, c])
        remote(got.at[c, y], got.at[c, y], send_y.at[1, c], recv_y.at[1, c], near)

    def go_forward(c):
        drain(other.at[c], recv_y.at[0, c])
        remote(got.at[c, 3 - y], got.at[c, 3 - y], send_y.at[2, c], recv_y.at[2, c], near)

    for c in range(CAP):
        go_z(c)
    go_x(0)
    go_x(1)
    go_y(0)
    go_x(2)
    go_y(1)
    go_forward(0)
    go_y(2)
    go_forward(1)
    go_forward(2)
    for c in range(CAP):
        for k in (1, 2):
            drain(other.at[c], recv_y.at[k, c])
        drain(stage.at[c, pl.ds(0, 15)], send_z.at[c])
        for k in range(2):
            drain(other.at[c, pl.ds(0, 3)], send_x.at[k, c])
        for k in range(3):
            drain(other.at[c], send_y.at[k, c])


def run_corner_turn(sent):
    vmem = pl.BlockSpec(memory_space=pltpu.VMEM)
    dma = pltpu.SemaphoreType.DMA
    return pl.pallas_call(
        corner_turn,
        out_shape=jax.ShapeDtypeStruct((CAP, 4, 4, 16, 3, 2, LANES), jnp.bfloat16),
        in_specs=[vmem],
        out_specs=vmem,
        scratch_shapes=[
            pltpu.VMEM((CAP, 16, 8, 3, 2, LANES), jnp.bfloat16),
            pltpu.VMEM((CAP, 4, 16, 3, 2, LANES), jnp.bfloat16),
            dma((CAP,)),
            dma((CAP,)),
            dma((2, CAP)),
            dma((2, CAP)),
            dma((3, CAP)),
            dma((3, CAP)),
            dma((3, CAP)),
        ],
        compiler_params=pltpu.CompilerParams(
            collective_id=0, has_side_effects=True, vmem_limit_bytes=16 * 1024 * 1024
        ),
        name="corner_turn",
    )(sent)


HALF = 512
TOTAL = 1024
CHUNK = 128


def correlate(got_ref, map_ref, count_ref, out_ref, places, rows_in, rows, wide):
    c = pl.program_id(0)
    part = pl.program_id(1)

    @pl.when((c == 0) & (part == 0))
    def _():
        want = lax.broadcasted_iota(jnp.int32, (TOTAL, LANES), 0)
        rows_in[...] = jnp.zeros_like(rows_in)
        for a in range(STREAMS):
            row = 2 * map_ref[a // 2 : a // 2 + 1, :] + a % 2
            places[:, a * LANES : (a + 1) * LANES] = jnp.where(want == row, 1.0, 0.0).astype(jnp.bfloat16)

    @pl.when(part == 0)
    def _():
        flat = got_ref.reshape(CAP, TOTAL * 3 // 2, LANES)
        wide[...] = flat[c].astype(jnp.float32)
        for p in range(2):
            for b in range(2):
                pieces = []
                for q in range(3):
                    first = wide[pl.ds(b * 384 + 2 * q + p, 64, stride=6), :]
                    second = wide[pl.ds((b + 2) * 384 + 2 * q + p, 64, stride=6), :]
                    pieces.append(jnp.concatenate([first, second], axis=0))
                line = jnp.concatenate(pieces, axis=1)
                for a in range(STREAMS):
                    lane = p * LANES + b * 64
                    rows_in[a * LANES : (a + 1) * LANES, lane : lane + NSPEC] = line[
                        :, a * NSPEC : (a + 1) * NSPEC
                    ].astype(jnp.bfloat16)
        rows[...] = jnp.dot(
            places[...], rows_in[...], preferred_element_type=jnp.float32
        ).astype(jnp.bfloat16)

    me = lax.axis_index("stn")
    lane = lax.broadcasted_iota(jnp.int32, (1, LANES), 1)
    live = jnp.sum(jnp.where(lane == me, count_ref[...], 0).astype(jnp.float32), axis=1, keepdims=True)
    scale = jnp.where(c.astype(jnp.float32) < live, 1.0 / (2 * NSPEC), 0.0)
    start = pl.multiple_of(lax.axis_index("blk") * HALF + part * CHUNK, CHUNK)
    mine = rows[pl.ds(start, CHUNK), :]
    turned = jnp.concatenate([mine[:, LANES:], -mine[:, :LANES]], axis=1)
    for k, left in enumerate((mine, turned)):
        product = lax.dot_general(
            left, rows[...], (((1,), (1,)), ((), ())), preferred_element_type=jnp.float32
        )
        out_ref[0, 0, k] = (product * scale).astype(jnp.bfloat16)


def run_correlate(got, station_map, chan_counts):
    by_source = station_map.reshape(4, 2, 16, 4).transpose(3, 1, 0, 2).reshape(4, LANES)
    return pl.pallas_call(
        correlate,
        grid=(CAP, HALF // CHUNK),
        out_shape=jax.ShapeDtypeStruct((1, CAP, 2, HALF, TOTAL), jnp.bfloat16),
        in_specs=[
            pl.BlockSpec((CAP, 4, 4, 16, 3, 2, LANES), lambda c, i: (0,) * 7),
            pl.BlockSpec((4, LANES), lambda c, i: (0, 0)),
            pl.BlockSpec((1, LANES), lambda c, i: (0, 0)),
        ],
        out_specs=pl.BlockSpec((1, 1, 2, CHUNK, TOTAL), lambda c, i: (0, c, 0, i, 0)),
        scratch_shapes=[
            pltpu.VMEM((TOTAL, TOTAL), jnp.bfloat16),
            pltpu.VMEM((TOTAL, 2 * LANES), jnp.bfloat16),
            pltpu.VMEM((TOTAL, 2 * LANES), jnp.bfloat16),
            pltpu.VMEM((TOTAL * 3 // 2, LANES), jnp.float32),
        ],
        compiler_params=pltpu.CompilerParams(vmem_limit_bytes=32 * 1024 * 1024),
        name="correlate",
    )(got, by_source, chan_counts.reshape(1, LANES))


def body(voltages, station_map, chan_counts):
    sent = run_channelize(voltages, chan_counts)
    got = run_corner_turn(sent)
    return run_correlate(got, station_map, chan_counts)


def solution(mesh):
    return jax.shard_map(
        body,
        mesh=mesh,
        in_specs=(P("stn", "blk", None, None, None), P(), P()),
        out_specs=P("stn", None, None, "blk", None),
        check_vma=False,
    )
```

```python
import functools
import math

import jax
import jax.numpy as jnp
import ml_dtypes
import numpy as np
from jax import lax
from jax.experimental import pallas as pl
from jax.experimental.pallas import tpu as pltpu
from jax.sharding import PartitionSpec as P

FFT_LEN = 4096
TAPS = 16
CAP = 3
NSPEC = 48
FRAMES = 63
STREAMS = 8
BAND = 256
LANES = 128
TILES = FFT_LEN // LANES
PARTS = 3
SPAN = NSPEC // PARTS
BLOCK = 16
ROWS = SPAN * STREAMS * 2
LAST = TAPS // 2
OUTER = sorted((t for t in range(TAPS) if t not in (LAST - 1, LAST)), key=lambda t: -abs(t - 7.5))
MESH = pl.DeviceIdType.MESH


def prototype():
    points = np.arange(TAPS * FFT_LEN) + 0.5
    span_len = TAPS * FFT_LEN
    filt = np.sinc((points - span_len / 2) / FFT_LEN) * (
        0.5 - 0.5 * np.cos(2.0 * math.pi * points / span_len)
    )
    filt = filt / np.sqrt(np.sum(filt * filt))
    return filt.reshape(TAPS, FFT_LEN)


def tables_of():
    filt = prototype()
    positions = np.arange(FFT_LEN)
    pivot = np.where(positions < FFT_LEN // 2, filt[LAST], filt[LAST - 1])
    ratios = (filt / pivot).reshape(TAPS, TILES, LANES).transpose(1, 0, 2)
    phase = (positions[:, None] * np.arange(BAND)[None, :] % FFT_LEN) * (2.0 * math.pi / FFT_LEN)
    table = np.concatenate([np.cos(phase), np.sin(phase)], axis=1) * pivot[:, None]
    return np.ascontiguousarray(ratios.astype(np.float32)), table.astype(ml_dtypes.bfloat16)


def fold_tile(tap_ref, frames, part, half, tile, lhs):
    pivot, partner = (LAST, LAST - 1) if half == 0 else (LAST - 1, LAST)
    taps = tap_ref[tile]
    low = {
        t: jnp.broadcast_to(taps[t : t + 1], (16, LANES)).astype(jnp.bfloat16)
        for t in [*OUTER, partner]
    }
    lanes = pl.ds(pl.multiple_of(tile * LANES, LANES), LANES)
    for base in range(0, SPAN, BLOCK):
        first = part * SPAN + base
        volts = [frames[first + r, tile] for r in range(BLOCK + TAPS - 1)]
        for s in range(BLOCK):
            small = low[OUTER[0]] * volts[s + OUTER[0]]
            for t in [*OUTER[1:], partner]:
                small = small + low[t] * volts[s + t]
            row = (base + s) * 16
            lhs[row : row + 16, lanes] = volts[s + pivot] + small


def choose_slots(count_ref, chosen):
    row = lax.broadcasted_iota(jnp.int32, (LANES, LANES), 0)
    device = (row & 7) * 16 + (row >> 3)
    lane = lax.broadcasted_iota(jnp.int32, (LANES, LANES), 1)
    counts = jnp.broadcast_to(count_ref[...], (LANES, LANES)).astype(jnp.float32)
    offset = jnp.sum(jnp.where(lane < device, counts, 0.0), axis=1, keepdims=True)
    count = jnp.sum(jnp.where(lane == device, counts, 0.0), axis=1, keepdims=True)
    band = lax.broadcasted_iota(jnp.int32, (LANES, BAND), 1)
    for k in range(CAP):
        pick = (offset + jnp.minimum(float(k), count - 1.0)).astype(jnp.int32)
        chosen[k] = jnp.where(band == pick, 1.0, 0.0).astype(jnp.bfloat16)


def transform(lhs, table, acc):
    got = jnp.dot(lhs[...], table[...], preferred_element_type=jnp.float32)
    for q in range(4):
        acc[q] = got[:, q * LANES : (q + 1) * LANES]


def outgoing(acc, chosen, spec, wide, out):
    for a in range(STREAMS):
        part = {}
        for p in range(2):
            for q in range(4):
                part[p, q] = acc[q, pl.ds(2 * a + p, SPAN, stride=16), :]
        for q in range(2):
            cols = slice(q * LANES, (q + 1) * LANES)
            rows = slice(a * SPAN, (a + 1) * SPAN)
            spec[0, rows, cols] = (part[0, q] + part[1, q + 2]).astype(jnp.bfloat16)
            spec[1, rows, cols] = (part[1, q] - part[0, q + 2]).astype(jnp.bfloat16)
    for k in range(CAP):
        for p in range(2):
            turned = lax.dot_general(
                chosen[k], spec[p], (((1,), (1,)), ((), ())), preferred_element_type=jnp.float32
            )
            wide[pl.ds(2 * k + p, LANES, stride=6), :] = turned
    out.reshape(LANES * 6, LANES)[...] = wide[...].astype(jnp.bfloat16)


def bring_in(volt_ref, out_ref, sems):
    copies = [
        pltpu.make_async_copy(volt_ref.at[a], out_ref.at[:, :, a], sems.at[a]) for a in range(STREAMS)
    ]
    for copy in copies:
        copy.start()
    for copy in copies:
        copy.wait()


def run_bring_in(voltages):
    tiles = voltages.reshape(STREAMS, FRAMES, 2, TILES, LANES).transpose(0, 1, 3, 2, 4)
    frames = pl.pallas_call(
        bring_in,
        out_shape=jax.ShapeDtypeStruct((FRAMES, TILES, STREAMS, 2, LANES), jnp.bfloat16),
        in_specs=[pl.BlockSpec(memory_space=pl.ANY)],
        out_specs=pl.BlockSpec(memory_space=pltpu.VMEM),
        scratch_shapes=[pltpu.SemaphoreType.DMA((STREAMS,))],
        compiler_params=pltpu.CompilerParams(vmem_limit_bytes=42 * 1024 * 1024),
        name="bring_in",
    )(tiles)
    return frames.reshape(FRAMES, TILES, 16, LANES)


class Filter:
    def __init__(self, frames, tap_ref, table, count_ref, lhs, acc, chosen, spec, wide):
        self.args = frames, tap_ref, table, count_ref, lhs, acc, chosen, spec, wide

    def start(self):
        choose_slots(self.args[3], self.args[6])

    def fold(self, part, half):
        frames, tap_ref, lhs = self.args[0], self.args[1], self.args[4]

        def step(i, carry):
            for u in range(2):
                fold_tile(tap_ref, frames, part, half, half * (TILES // 2) + 2 * i + u, lhs)
            return carry

        lax.fori_loop(0, TILES // 4, step, 0)

    def finish(self, out):
        _, _, table, _, lhs, acc, chosen, spec, wide = self.args
        transform(lhs, table, acc)
        outgoing(acc, chosen, spec, wide, out)


FILTER_SCRATCH = [
    pltpu.VMEM((ROWS, FFT_LEN), jnp.bfloat16),
    pltpu.VMEM((4, ROWS, LANES), jnp.float32),
    pltpu.VMEM((CAP, LANES, BAND), jnp.bfloat16),
    pltpu.VMEM((2, ROWS // 2, BAND), jnp.bfloat16),
    pltpu.VMEM((LANES * 6, LANES), jnp.float32),
]


def filter_and_turn(frames, tap_ref, table, count_ref, got, lhs, acc, chosen, spec, wide, sent, stage, other, send_z, recv_z, send_x, recv_x, send_y, recv_y, local_sems):
    stn = lax.axis_index("stn")
    blk = lax.axis_index("blk")
    g = lax.rem(stn, 16)
    h = lax.div(stn, 16)
    x = lax.div(h, 2)
    y_hi = lax.rem(h, 2)
    y = 2 * y_hi + blk

    def at(x_to, y_hi_to, g_to):
        return (x_to * 2 + y_hi_to) * 16 + g_to

    near = {"stn": stn, "blk": 1 - blk}
    cross = {"stn": at(x, 1 - y_hi, g), "blk": 1 - blk}
    ring_z = [{"stn": at(x, y_hi, lax.rem(g + j, 16)), "blk": blk} for j in range(1, 16)]
    ring_x = [{"stn": at(lax.rem(x + j, 4), y_hi, g), "blk": blk} for j in range(1, 4)]

    barrier = pltpu.get_barrier_semaphore()
    partners = [*ring_z, *ring_x, near, cross]
    for partner in partners:
        pl.semaphore_signal(barrier, inc=1, device_id=partner, device_id_type=MESH)
    bank = Filter(frames, tap_ref, table, count_ref, lhs, acc, chosen, spec, wide)

    def remote(src, dst, send, recv, device):
        copy = pltpu.make_async_remote_copy(
            src_ref=src, dst_ref=dst, send_sem=send, recv_sem=recv, device_id=device, device_id_type=MESH
        )
        copy.start()

    def drain(ref, sem):
        pltpu.make_async_copy(ref, ref, sem).wait()

    def own_z(c):
        return pltpu.make_async_copy(sent.at[c, g], stage.at[c, g], local_sems.at[0, c])

    def own_x(c, half):
        if half == 0:
            return pltpu.make_async_copy(
                stage.at[c, :, x * 2 + y_hi], got.at[c, y, x], local_sems.at[1, c]
            )
        return pltpu.make_async_copy(
            stage.at[c, :, x * 2 + 1 - y_hi], other.at[c, x], local_sems.at[2, c]
        )

    def go_z(c):
        own_z(c).start()
        for j in range(1, 16):
            remote(
                sent.at[c, lax.rem(g + j, 16)], stage.at[c, g], send_z.at[c], recv_z.at[c], ring_z[j - 1]
            )

    def go_x(c):
        own_z(c).wait()
        drain(stage.at[c, pl.ds(0, 15)], recv_z.at[c])
        own_x(c, 0).start()
        own_x(c, 1).start()
        for j in range(1, 4):
            x_to = lax.rem(x + j, 4)
            remote(
                stage.at[c, :, x_to * 2 + 1 - y_hi], other.at[c, x], send_x.at[1, c], recv_x.at[1, c], ring_x[j - 1]
            )
        for j in range(1, 4):
            x_to = lax.rem(x + j, 4)
            remote(
                stage.at[c, :, x_to * 2 + y_hi], got.at[c, y, x], send_x.at[0, c], recv_x.at[0, c], ring_x[j - 1]
            )

    def go_y(c):
        own_x(c, 1).wait()
        drain(other.at[c, pl.ds(0, 3)], recv_x.at[1, c])
        remote(other.at[c], got.at[c, y], send_y.at[0, c], recv_y.at[0, c], cross)
        own_x(c, 0).wait()
        drain(other.at[c, pl.ds(0, 3)], recv_x.at[0, c])
        remote(got.at[c, y], got.at[c, y], send_y.at[1, c], recv_y.at[1, c], near)

    def go_forward(c):
        drain(other.at[c], recv_y.at[0, c])
        remote(got.at[c, 3 - y], got.at[c, 3 - y], send_y.at[2, c], recv_y.at[2, c], near)

    bank.start()
    bank.fold(0, 0)
    bank.fold(0, 1)
    bank.finish(sent.at[0])
    pl.semaphore_wait(barrier, len(partners))
    go_z(0)
    bank.fold(1, 0)
    bank.fold(1, 1)
    bank.finish(sent.at[1])
    go_z(1)
    bank.fold(2, 0)
    go_x(0)
    bank.fold(2, 1)
    bank.finish(sent.at[2])
    go_z(2)
    go_y(0)
    go_x(1)
    go_forward(0)
    go_y(1)
    go_x(2)
    go_forward(1)
    go_y(2)
    go_forward(2)
    for c in range(PARTS):
        for k in (1, 2):
            drain(other.at[c], recv_y.at[k, c])
        drain(stage.at[c, pl.ds(0, 15)], send_z.at[c])
        for k in range(2):
            drain(other.at[c, pl.ds(0, 3)], send_x.at[k, c])
        for k in range(3):
            drain(other.at[c], send_y.at[k, c])


def run_filter_and_turn(voltages, chan_counts):
    vmem = pl.BlockSpec(memory_space=pltpu.VMEM)
    dma = pltpu.SemaphoreType.DMA
    ratios, table = tables_of()
    return pl.pallas_call(
        filter_and_turn,
        out_shape=jax.ShapeDtypeStruct((PARTS, 4, 4, 16, CAP, 2, LANES), jnp.bfloat16),
        in_specs=[vmem] * 4,
        out_specs=vmem,
        scratch_shapes=[
            *FILTER_SCRATCH,
            pltpu.VMEM((PARTS, 16, 8, CAP, 2, LANES), jnp.bfloat16),
            pltpu.VMEM((PARTS, 16, 8, CAP, 2, LANES), jnp.bfloat16),
            pltpu.VMEM((PARTS, 4, 16, CAP, 2, LANES), jnp.bfloat16),
            dma((PARTS,)),
            dma((PARTS,)),
            dma((2, PARTS)),
            dma((2, PARTS)),
            dma((3, PARTS)),
            dma((3, PARTS)),
            dma((3, PARTS)),
        ],
        compiler_params=pltpu.CompilerParams(
            collective_id=0, has_side_effects=True, vmem_limit_bytes=16 * 1024 * 1024
        ),
        name="filter_and_turn",
    )(run_bring_in(voltages), jnp.asarray(ratios), jnp.asarray(table), chan_counts.reshape(1, LANES))


HALF = 512
TOTAL = 1024
CHUNK = 128
TIMES = 2 * NSPEC


def correlate(got_ref, map_ref, count_ref, out_ref, places, wide, lines, columns, mine, turned):
    k = pl.program_id(0)
    part = pl.program_id(1)

    @pl.when((k == 0) & (part == 0))
    def _():
        want = lax.broadcasted_iota(jnp.int32, (LANES, TOTAL), 1)
        for a in range(STREAMS):
            row = 2 * map_ref[:, a // 2 : a // 2 + 1] + a % 2
            places[a * LANES : (a + 1) * LANES, :] = jnp.where(want == row, 1.0, 0.0).astype(jnp.bfloat16)
        wide[...] = got_ref[...].astype(jnp.float32)

    @pl.when(part == 0)
    def _():
        for p in range(2):
            for b in range(2):
                for t in range(PARTS):
                    base = t * 1536 + 2 * k + p
                    first = wide[pl.ds(base + b * 384, 64, stride=6), :]
                    second = wide[pl.ds(base + (b + 2) * 384, 64, stride=6), :]
                    block = jnp.concatenate([first, second], axis=0).T.astype(jnp.bfloat16)
                    row = p * TIMES + b * NSPEC + t * SPAN
                    for a in range(STREAMS):
                        lines[row : row + SPAN, a * LANES : (a + 1) * LANES] = block[
                            a * SPAN : (a + 1) * SPAN
                        ]
        ordered = jnp.dot(lines[...], places[...], preferred_element_type=jnp.float32)
        columns[...] = ordered.astype(jnp.bfloat16)
        start = pl.multiple_of(lax.axis_index("blk") * HALF, HALF)
        near = columns[:, pl.ds(start, HALF)].astype(jnp.float32)
        mine[...] = near.T.astype(jnp.bfloat16)
        turned[...] = jnp.concatenate([near[TIMES:], -near[:TIMES]], axis=0).T.astype(jnp.bfloat16)

    me = lax.axis_index("stn")
    lane = lax.broadcasted_iota(jnp.int32, (1, LANES), 1)
    live = jnp.sum(jnp.where(lane == me, count_ref[...], 0).astype(jnp.float32), axis=1, keepdims=True)
    scale = jnp.where(k.astype(jnp.float32) < live, 1.0 / TIMES, 0.0)
    rows = pl.ds(pl.multiple_of(part * CHUNK, CHUNK), CHUNK)
    for i, left in enumerate((mine, turned)):
        product = jnp.dot(left[rows, :], columns[...], preferred_element_type=jnp.float32)
        out_ref[0, 0, i] = (product * scale).astype(jnp.bfloat16)


def run_correlate(got, station_map, chan_counts):
    by_source = station_map.reshape(4, 2, 16, 4).transpose(1, 0, 2, 3).reshape(LANES, 4)
    return pl.pallas_call(
        correlate,
        grid=(CAP, HALF // CHUNK),
        out_shape=jax.ShapeDtypeStruct((1, CAP, 2, HALF, TOTAL), jnp.bfloat16),
        in_specs=[
            pl.BlockSpec((PARTS * TOTAL * 3 // 2, LANES), lambda k, i: (0, 0)),
            pl.BlockSpec((LANES, 4), lambda k, i: (0, 0)),
            pl.BlockSpec((1, LANES), lambda k, i: (0, 0)),
        ],
        out_specs=pl.BlockSpec((1, 1, 2, CHUNK, TOTAL), lambda k, i: (0, k, 0, i, 0)),
        scratch_shapes=[
            pltpu.VMEM((TOTAL, TOTAL), jnp.bfloat16),
            pltpu.VMEM((PARTS * TOTAL * 3 // 2, LANES), jnp.float32),
            pltpu.VMEM((2 * TIMES, TOTAL), jnp.bfloat16),
            pltpu.VMEM((2 * TIMES, TOTAL), jnp.bfloat16),
            pltpu.VMEM((HALF, 2 * TIMES), jnp.bfloat16),
            pltpu.VMEM((HALF, 2 * TIMES), jnp.bfloat16),
        ],
        compiler_params=pltpu.CompilerParams(vmem_limit_bytes=32 * 1024 * 1024),
        name="correlate",
    )(got.reshape(PARTS * TOTAL * 3 // 2, LANES), by_source, chan_counts.reshape(1, LANES))


def body(voltages, station_map, chan_counts):
    got = run_filter_and_turn(voltages, chan_counts)
    return run_correlate(got, station_map, chan_counts)


def solution(mesh):
    return jax.shard_map(
        body,
        mesh=mesh,
        in_specs=(P("stn", "blk", None, None, None), P(), P()),
        out_specs=P("stn", None, None, "blk", None),
        check_vma=False,
    )
```

```python
import functools
import math

import jax
import jax.numpy as jnp
import ml_dtypes
import numpy as np
from jax import lax
from jax.experimental import pallas as pl
from jax.experimental.pallas import tpu as pltpu
from jax.sharding import PartitionSpec as P

FFT_LEN = 4096
TAPS = 16
CAP = 3
NSPEC = 48
FRAMES = 63
STREAMS = 8
BAND = 256
LANES = 128
TILES = FFT_LEN // LANES
PARTS = 3
SPAN = NSPEC // PARTS
BLOCK = 16
ROWS = SPAN * STREAMS * 2
LAST = TAPS // 2
OUTER = sorted((t for t in range(TAPS) if t not in (LAST - 1, LAST)), key=lambda t: -abs(t - 7.5))
MESH = pl.DeviceIdType.MESH


def prototype():
    points = np.arange(TAPS * FFT_LEN) + 0.5
    span_len = TAPS * FFT_LEN
    filt = np.sinc((points - span_len / 2) / FFT_LEN) * (
        0.5 - 0.5 * np.cos(2.0 * math.pi * points / span_len)
    )
    filt = filt / np.sqrt(np.sum(filt * filt))
    return filt.reshape(TAPS, FFT_LEN)


def tables_of():
    filt = prototype()
    positions = np.arange(FFT_LEN)
    pivot = np.where(positions < FFT_LEN // 2, filt[LAST], filt[LAST - 1])
    ratios = (filt / pivot).reshape(TAPS, TILES, LANES).transpose(1, 0, 2)
    phase = (positions[:, None] * np.arange(BAND)[None, :] % FFT_LEN) * (2.0 * math.pi / FFT_LEN)
    table = np.concatenate([np.cos(phase), np.sin(phase)], axis=1) * pivot[:, None]
    return np.ascontiguousarray(ratios.astype(np.float32)), table.astype(ml_dtypes.bfloat16)


def fold_tile(tap_ref, frames, part, half, tile, lhs):
    pivot, partner = (LAST, LAST - 1) if half == 0 else (LAST - 1, LAST)
    taps = tap_ref[tile]
    low = {
        t: jnp.broadcast_to(taps[t : t + 1], (16, LANES)).astype(jnp.bfloat16)
        for t in [*OUTER, partner]
    }
    lanes = pl.ds(pl.multiple_of(tile * LANES, LANES), LANES)
    for base in range(0, SPAN, BLOCK):
        first = part * SPAN + base
        volts = [frames[first + r, tile] for r in range(BLOCK + TAPS - 1)]
        for s in range(BLOCK):
            small = low[OUTER[0]] * volts[s + OUTER[0]]
            for t in [*OUTER[1:], partner]:
                small = small + low[t] * volts[s + t]
            row = (base + s) * 16
            lhs[row : row + 16, lanes] = volts[s + pivot] + small


def choose_slots(count_ref, chosen):
    row = lax.broadcasted_iota(jnp.int32, (LANES, LANES), 0)
    device = (row & 7) * 16 + (row >> 3)
    lane = lax.broadcasted_iota(jnp.int32, (LANES, LANES), 1)
    counts = jnp.broadcast_to(count_ref[...], (LANES, LANES)).astype(jnp.float32)
    offset = jnp.sum(jnp.where(lane < device, counts, 0.0), axis=1, keepdims=True)
    count = jnp.sum(jnp.where(lane == device, counts, 0.0), axis=1, keepdims=True)
    band = lax.broadcasted_iota(jnp.int32, (LANES, BAND), 1)
    for k in range(CAP):
        pick = (offset + jnp.minimum(float(k), count - 1.0)).astype(jnp.int32)
        chosen[k] = jnp.where(band == pick, 1.0, 0.0).astype(jnp.bfloat16)


def transform(lhs, table, acc):
    got = jnp.dot(lhs[...], table[...], preferred_element_type=jnp.float32)
    for q in range(4):
        acc[q] = got[:, q * LANES : (q + 1) * LANES]


def outgoing(acc, chosen, spec, wide, out):
    for a in range(STREAMS):
        part = {}
        for p in range(2):
            for q in range(4):
                part[p, q] = acc[q, pl.ds(2 * a + p, SPAN, stride=16), :]
        for q in range(2):
            cols = slice(q * LANES, (q + 1) * LANES)
            rows = slice(a * SPAN, (a + 1) * SPAN)
            spec[0, rows, cols] = (part[0, q] + part[1, q + 2]).astype(jnp.bfloat16)
            spec[1, rows, cols] = (part[1, q] - part[0, q + 2]).astype(jnp.bfloat16)
    for k in range(CAP):
        for p in range(2):
            turned = lax.dot_general(
                chosen[k], spec[p], (((1,), (1,)), ((), ())), preferred_element_type=jnp.float32
            )
            wide[pl.ds(2 * k + p, LANES, stride=6), :] = turned
    out.reshape(LANES * 6, LANES)[...] = wide[...].astype(jnp.bfloat16)


def bring_in(volt_ref, out_ref, sems):
    copies = [
        pltpu.make_async_copy(volt_ref.at[a], out_ref.at[:, :, a], sems.at[a]) for a in range(STREAMS)
    ]
    for copy in copies:
        copy.start()
    for copy in copies:
        copy.wait()


def run_bring_in(voltages):
    tiles = voltages.reshape(STREAMS, FRAMES, 2, TILES, LANES).transpose(0, 1, 3, 2, 4)
    frames = pl.pallas_call(
        bring_in,
        out_shape=jax.ShapeDtypeStruct((FRAMES, TILES, STREAMS, 2, LANES), jnp.bfloat16),
        in_specs=[pl.BlockSpec(memory_space=pl.ANY)],
        out_specs=pl.BlockSpec(memory_space=pltpu.VMEM),
        scratch_shapes=[pltpu.SemaphoreType.DMA((STREAMS,))],
        compiler_params=pltpu.CompilerParams(vmem_limit_bytes=42 * 1024 * 1024),
        name="bring_in",
    )(tiles)
    return frames.reshape(FRAMES, TILES, 16, LANES)


class Filter:
    def __init__(self, frames, tap_ref, table, count_ref, lhs, acc, chosen, spec, wide):
        self.args = frames, tap_ref, table, count_ref, lhs, acc, chosen, spec, wide

    def start(self):
        choose_slots(self.args[3], self.args[6])

    def fold(self, part, half):
        frames, tap_ref, lhs = self.args[0], self.args[1], self.args[4]

        def step(i, carry):
            for u in range(2):
                fold_tile(tap_ref, frames, part, half, half * (TILES // 2) + 2 * i + u, lhs)
            return carry

        lax.fori_loop(0, TILES // 4, step, 0)

    def finish(self, out):
        _, _, table, _, lhs, acc, chosen, spec, wide = self.args
        transform(lhs, table, acc)
        outgoing(acc, chosen, spec, wide, out)


FILTER_SCRATCH = [
    pltpu.VMEM((ROWS, FFT_LEN), jnp.bfloat16),
    pltpu.VMEM((4, ROWS, LANES), jnp.float32),
    pltpu.VMEM((CAP, LANES, BAND), jnp.bfloat16),
    pltpu.VMEM((2, ROWS // 2, BAND), jnp.bfloat16),
    pltpu.VMEM((LANES * 6, LANES), jnp.float32),
]


HALF = 512
TOTAL = 1024
TIMES = 2 * NSPEC
LINES = TOTAL * 3 // 2


def build_places(map_ref, places):
    row = lax.broadcasted_iota(jnp.int32, (LANES, LANES), 0)
    lane = lax.broadcasted_iota(jnp.int32, (LANES, LANES), 1)
    listed = jnp.zeros((LANES, LANES), jnp.float32)
    for x in range(4):
        stations = jnp.broadcast_to(map_ref[x : x + 1, :], (LANES, LANES)).astype(jnp.float32)
        listed = jnp.where(((row >> 4) & 3) == x, stations, listed)
    first = (row >> 6) * 64 + (row & 15) * 4
    want = lax.broadcasted_iota(jnp.int32, (LANES, TOTAL), 1)
    for pair in range(4):
        station = jnp.sum(jnp.where(lane == first + pair, listed, 0.0), axis=1, keepdims=True)
        for p in range(2):
            a = 2 * pair + p
            target = 2 * station.astype(jnp.int32) + p
            places[a * LANES : (a + 1) * LANES, :] = jnp.where(want == target, 1.0, 0.0).astype(jnp.bfloat16)


def order_rows(part, got, places, gathered, lines, columns):
    gathered[...] = got.reshape(LINES, LANES)[...].astype(jnp.float32)
    spots = [(k, p, b) for k in range(CAP) for p in range(2) for b in range(2)]
    for i, (k, p, b) in enumerate(spots):
        base = 2 * k + p
        first = gathered[pl.ds(base + b * 384, 64, stride=6), :]
        second = gathered[pl.ds(base + (b + 2) * 384, 64, stride=6), :]
        block = jnp.concatenate([first, second], axis=0).T.astype(jnp.bfloat16)
        for a in range(STREAMS):
            lines[i * SPAN : (i + 1) * SPAN, a * LANES : (a + 1) * LANES] = block[a * SPAN : (a + 1) * SPAN]
    ordered = jnp.dot(lines[...], places[...], preferred_element_type=jnp.float32)
    for i, (k, p, b) in enumerate(spots):
        row = p * TIMES + b * NSPEC + part * SPAN
        columns[k, row : row + SPAN, :] = ordered[i * SPAN : (i + 1) * SPAN].astype(jnp.bfloat16)


def filter_and_turn(
    frames, tap_ref, table, count_ref, map_ref, columns, lhs, acc, chosen, spec, wide, places, gathered,
    lines, got, sent, stage, other, send_z, recv_z, send_x, recv_x, send_y, recv_y, local_sems
):
    stn = lax.axis_index("stn")
    blk = lax.axis_index("blk")
    g = lax.rem(stn, 16)
    h = lax.div(stn, 16)
    x = lax.div(h, 2)
    y_hi = lax.rem(h, 2)
    y = 2 * y_hi + blk

    def at(x_to, y_hi_to, g_to):
        return (x_to * 2 + y_hi_to) * 16 + g_to

    near = {"stn": stn, "blk": 1 - blk}
    cross = {"stn": at(x, 1 - y_hi, g), "blk": 1 - blk}
    ring_z = [{"stn": at(x, y_hi, lax.rem(g + j, 16)), "blk": blk} for j in range(1, 16)]
    ring_x = [{"stn": at(lax.rem(x + j, 4), y_hi, g), "blk": blk} for j in range(1, 4)]

    barrier = pltpu.get_barrier_semaphore()
    partners = [*ring_z, *ring_x, near, cross]
    for partner in partners:
        pl.semaphore_signal(barrier, inc=1, device_id=partner, device_id_type=MESH)
    bank = Filter(frames, tap_ref, table, count_ref, lhs, acc, chosen, spec, wide)

    def remote(src, dst, send, recv, device):
        copy = pltpu.make_async_remote_copy(
            src_ref=src, dst_ref=dst, send_sem=send, recv_sem=recv, device_id=device, device_id_type=MESH
        )
        copy.start()

    def drain(ref, sem):
        pltpu.make_async_copy(ref, ref, sem).wait()

    def own_z(c):
        return pltpu.make_async_copy(sent.at[c, g], stage.at[c, g], local_sems.at[0, c])

    def own_x(c, half):
        if half == 0:
            return pltpu.make_async_copy(
                stage.at[c, :, x * 2 + y_hi], got.at[c, y, x], local_sems.at[1, c]
            )
        return pltpu.make_async_copy(
            stage.at[c, :, x * 2 + 1 - y_hi], other.at[c, x], local_sems.at[2, c]
        )

    def go_z(c):
        own_z(c).start()
        for j in range(1, 16):
            remote(
                sent.at[c, lax.rem(g + j, 16)], stage.at[c, g], send_z.at[c], recv_z.at[c], ring_z[j - 1]
            )

    def go_x(c):
        own_z(c).wait()
        drain(stage.at[c, pl.ds(0, 15)], recv_z.at[c])
        own_x(c, 0).start()
        own_x(c, 1).start()
        for j in range(1, 4):
            x_to = lax.rem(x + j, 4)
            remote(
                stage.at[c, :, x_to * 2 + 1 - y_hi], other.at[c, x], send_x.at[1, c], recv_x.at[1, c], ring_x[j - 1]
            )
        for j in range(1, 4):
            x_to = lax.rem(x + j, 4)
            remote(
                stage.at[c, :, x_to * 2 + y_hi], got.at[c, y, x], send_x.at[0, c], recv_x.at[0, c], ring_x[j - 1]
            )

    def go_y(c):
        own_x(c, 1).wait()
        drain(other.at[c, pl.ds(0, 3)], recv_x.at[1, c])
        remote(other.at[c], got.at[c, y], send_y.at[0, c], recv_y.at[0, c], cross)
        own_x(c, 0).wait()
        drain(other.at[c, pl.ds(0, 3)], recv_x.at[0, c])
        remote(got.at[c, y], got.at[c, y], send_y.at[1, c], recv_y.at[1, c], near)

    def go_forward(c):
        drain(other.at[c], recv_y.at[0, c])
        remote(got.at[c, 3 - y], got.at[c, 3 - y], send_y.at[2, c], recv_y.at[2, c], near)

    def order(c):
        drain(other.at[c], recv_y.at[1, c])
        drain(other.at[c], recv_y.at[2, c])
        order_rows(c, got.at[c], places, gathered, lines, columns)

    bank.start()
    bank.fold(0, 0)
    bank.fold(0, 1)
    bank.finish(sent.at[0])
    pl.semaphore_wait(barrier, len(partners))
    go_z(0)
    bank.fold(1, 0)
    bank.fold(1, 1)
    bank.finish(sent.at[1])
    go_z(1)
    bank.fold(2, 0)
    go_x(0)
    bank.fold(2, 1)
    bank.finish(sent.at[2])
    go_z(2)
    go_y(0)
    build_places(map_ref, places)
    go_x(1)
    go_forward(0)
    go_y(1)
    go_x(2)
    go_forward(1)
    go_y(2)
    go_forward(2)
    for c in range(PARTS):
        order(c)
    for c in range(PARTS):
        drain(stage.at[c, pl.ds(0, 15)], send_z.at[c])
        for k in range(2):
            drain(other.at[c, pl.ds(0, 3)], send_x.at[k, c])
        for k in range(3):
            drain(other.at[c], send_y.at[k, c])


def run_filter_and_turn(voltages, station_map, chan_counts):
    vmem = pl.BlockSpec(memory_space=pltpu.VMEM)
    dma = pltpu.SemaphoreType.DMA
    ratios, table = tables_of()
    return pl.pallas_call(
        filter_and_turn,
        out_shape=jax.ShapeDtypeStruct((CAP, 2 * TIMES, TOTAL), jnp.bfloat16),
        in_specs=[vmem] * 5,
        out_specs=vmem,
        scratch_shapes=[
            *FILTER_SCRATCH,
            pltpu.VMEM((TOTAL, TOTAL), jnp.bfloat16),
            pltpu.VMEM((LINES, LANES), jnp.float32),
            pltpu.VMEM((12 * SPAN, TOTAL), jnp.bfloat16),
            pltpu.VMEM((PARTS, 4, 4, 16, CAP, 2, LANES), jnp.bfloat16),
            pltpu.VMEM((PARTS, 16, 8, CAP, 2, LANES), jnp.bfloat16),
            pltpu.VMEM((PARTS, 16, 8, CAP, 2, LANES), jnp.bfloat16),
            pltpu.VMEM((PARTS, 4, 16, CAP, 2, LANES), jnp.bfloat16),
            dma((PARTS,)),
            dma((PARTS,)),
            dma((2, PARTS)),
            dma((2, PARTS)),
            dma((3, PARTS)),
            dma((3, PARTS)),
            dma((3, PARTS)),
        ],
        compiler_params=pltpu.CompilerParams(
            collective_id=0, has_side_effects=True, vmem_limit_bytes=24 * 1024 * 1024
        ),
        name="filter_and_turn",
    )(
        run_bring_in(voltages),
        jnp.asarray(ratios),
        jnp.asarray(table),
        chan_counts.reshape(1, LANES),
        station_map.reshape(4, LANES),
    )


COLUMNS = 512


def correlate(columns, count_ref, out_ref, left):
    k = pl.program_id(0)
    part = pl.program_id(1)

    @pl.when(part == 0)
    def _():
        start = pl.multiple_of(lax.axis_index("blk") * HALF, HALF)
        mine = columns[k, :, pl.ds(start, HALF)]
        left[:HALF, :] = mine.T
        left[HALF:, :] = jnp.concatenate([mine[TIMES:], -mine[:TIMES]], axis=0).T

    me = lax.axis_index("stn")
    lane = lax.broadcasted_iota(jnp.int32, (1, LANES), 1)
    live = jnp.sum(jnp.where(lane == me, count_ref[...], 0).astype(jnp.float32), axis=1, keepdims=True)
    scale = jnp.where(k.astype(jnp.float32) < live, 1.0 / TIMES, 0.0)
    for n in range(COLUMNS // 256):
        right = columns[k, :, pl.ds(pl.multiple_of(part * COLUMNS + n * 256, 256), 256)]
        for i in range(2):
            product = jnp.dot(left[i * HALF : (i + 1) * HALF], right, preferred_element_type=jnp.float32)
            out_ref[0, 0, i, :, n * 256 : (n + 1) * 256] = (product * scale).astype(jnp.bfloat16)


def run_correlate(columns, chan_counts):
    return pl.pallas_call(
        correlate,
        grid=(CAP, TOTAL // COLUMNS),
        out_shape=jax.ShapeDtypeStruct((1, CAP, 2, HALF, TOTAL), jnp.bfloat16),
        in_specs=[
            pl.BlockSpec(memory_space=pltpu.VMEM),
            pl.BlockSpec(memory_space=pltpu.VMEM),
        ],
        out_specs=pl.BlockSpec((1, 1, 2, HALF, COLUMNS), lambda k, i: (0, k, 0, 0, i)),
        scratch_shapes=[pltpu.VMEM((TOTAL, 2 * TIMES), jnp.bfloat16)],
        compiler_params=pltpu.CompilerParams(vmem_limit_bytes=32 * 1024 * 1024),
        name="correlate",
    )(columns, chan_counts.reshape(1, LANES))


def body(voltages, station_map, chan_counts):
    columns = run_filter_and_turn(voltages, station_map, chan_counts)
    return run_correlate(columns, chan_counts)


def solution(mesh):
    return jax.shard_map(
        body,
        mesh=mesh,
        in_specs=(P("stn", "blk", None, None, None), P(), P()),
        out_specs=P("stn", None, None, "blk", None),
        check_vma=False,
    )
```

```python
import functools
import math

import jax
import jax.numpy as jnp
import ml_dtypes
import numpy as np
from jax import lax
from jax.experimental import pallas as pl
from jax.experimental.pallas import tpu as pltpu
from jax.sharding import PartitionSpec as P

FFT_LEN = 4096
TAPS = 16
CAP = 3
NSPEC = 48
FRAMES = 63
STREAMS = 8
BAND = 256
LANES = 128
TILES = FFT_LEN // LANES
PARTS = 3
SPAN = NSPEC // PARTS
BLOCK = 16
ROWS = SPAN * STREAMS * 2
LAST = TAPS // 2
OUTER = sorted((t for t in range(TAPS) if t not in (LAST - 1, LAST)), key=lambda t: -abs(t - 7.5))
MESH = pl.DeviceIdType.MESH


def prototype():
    points = np.arange(TAPS * FFT_LEN) + 0.5
    span_len = TAPS * FFT_LEN
    filt = np.sinc((points - span_len / 2) / FFT_LEN) * (
        0.5 - 0.5 * np.cos(2.0 * math.pi * points / span_len)
    )
    filt = filt / np.sqrt(np.sum(filt * filt))
    return filt.reshape(TAPS, FFT_LEN)


def tables_of():
    filt = prototype()
    positions = np.arange(FFT_LEN)
    pivot = np.where(positions < FFT_LEN // 2, filt[LAST], filt[LAST - 1])
    ratios = (filt / pivot).reshape(TAPS, TILES, LANES).transpose(1, 0, 2)
    phase = (positions[:, None] * np.arange(BAND)[None, :] % FFT_LEN) * (2.0 * math.pi / FFT_LEN)
    table = np.concatenate([np.cos(phase), np.sin(phase)], axis=1) * pivot[:, None]
    return np.ascontiguousarray(ratios.astype(np.float32)), table.astype(ml_dtypes.bfloat16)


def fold_tile(tap_ref, frames, part, half, tile, lhs):
    pivot, partner = (LAST, LAST - 1) if half == 0 else (LAST - 1, LAST)
    taps = tap_ref[tile]
    low = {
        t: jnp.broadcast_to(taps[t : t + 1], (16, LANES)).astype(jnp.bfloat16)
        for t in [*OUTER, partner]
    }
    lanes = pl.ds(pl.multiple_of(tile * LANES, LANES), LANES)
    for base in range(0, SPAN, BLOCK):
        first = part * SPAN + base
        volts = [frames[first + r, tile] for r in range(BLOCK + TAPS - 1)]
        for s in range(BLOCK):
            small = low[OUTER[0]] * volts[s + OUTER[0]]
            for t in [*OUTER[1:], partner]:
                small = small + low[t] * volts[s + t]
            row = (base + s) * 16
            lhs[row : row + 16, lanes] = volts[s + pivot] + small


def choose_slots(count_ref, chosen):
    row = lax.broadcasted_iota(jnp.int32, (LANES, LANES), 0)
    device = (row & 7) * 16 + (row >> 3)
    lane = lax.broadcasted_iota(jnp.int32, (LANES, LANES), 1)
    counts = jnp.broadcast_to(count_ref[...], (LANES, LANES)).astype(jnp.float32)
    offset = jnp.sum(jnp.where(lane < device, counts, 0.0), axis=1, keepdims=True)
    count = jnp.sum(jnp.where(lane == device, counts, 0.0), axis=1, keepdims=True)
    band = lax.broadcasted_iota(jnp.int32, (LANES, BAND), 1)
    for k in range(CAP):
        pick = (offset + jnp.minimum(float(k), count - 1.0)).astype(jnp.int32)
        chosen[k] = jnp.where(band == pick, 1.0, 0.0).astype(jnp.bfloat16)


def transform(lhs, table, acc):
    got = jnp.dot(lhs[...], table[...], preferred_element_type=jnp.float32)
    for q in range(4):
        acc[q] = got[:, q * LANES : (q + 1) * LANES]


def outgoing(acc, chosen, spec, wide, out):
    for a in range(STREAMS):
        part = {}
        for p in range(2):
            for q in range(4):
                part[p, q] = acc[q, pl.ds(2 * a + p, SPAN, stride=16), :]
        for q in range(2):
            cols = slice(q * LANES, (q + 1) * LANES)
            rows = slice(a * SPAN, (a + 1) * SPAN)
            spec[0, rows, cols] = (part[0, q] + part[1, q + 2]).astype(jnp.bfloat16)
            spec[1, rows, cols] = (part[1, q] - part[0, q + 2]).astype(jnp.bfloat16)
    for k in range(CAP):
        for p in range(2):
            turned = lax.dot_general(
                chosen[k], spec[p], (((1,), (1,)), ((), ())), preferred_element_type=jnp.float32
            )
            wide[pl.ds(2 * k + p, LANES, stride=6), :] = turned
    out.reshape(LANES * 6, LANES)[...] = wide[...].astype(jnp.bfloat16)


def bring_in(volt_ref, out_ref, sems):
    copies = [
        pltpu.make_async_copy(volt_ref.at[a], out_ref.at[:, :, a], sems.at[a]) for a in range(STREAMS)
    ]
    for copy in copies:
        copy.start()
    for copy in copies:
        copy.wait()


def run_bring_in(voltages):
    tiles = voltages.reshape(STREAMS, FRAMES, 2, TILES, LANES).transpose(0, 1, 3, 2, 4)
    frames = pl.pallas_call(
        bring_in,
        out_shape=jax.ShapeDtypeStruct((FRAMES, TILES, STREAMS, 2, LANES), jnp.bfloat16),
        in_specs=[pl.BlockSpec(memory_space=pl.ANY)],
        out_specs=pl.BlockSpec(memory_space=pltpu.VMEM),
        scratch_shapes=[pltpu.SemaphoreType.DMA((STREAMS,))],
        compiler_params=pltpu.CompilerParams(vmem_limit_bytes=42 * 1024 * 1024),
        name="bring_in",
    )(tiles)
    return frames.reshape(FRAMES, TILES, 16, LANES)


class Filter:
    def __init__(self, frames, tap_ref, table, count_ref, lhs, acc, chosen, spec, wide):
        self.args = frames, tap_ref, table, count_ref, lhs, acc, chosen, spec, wide

    def start(self):
        choose_slots(self.args[3], self.args[6])

    def fold(self, part, half):
        frames, tap_ref, lhs = self.args[0], self.args[1], self.args[4]

        def step(i, carry):
            for u in range(2):
                fold_tile(tap_ref, frames, part, half, half * (TILES // 2) + 2 * i + u, lhs)
            return carry

        lax.fori_loop(0, TILES // 4, step, 0)

    def finish(self, out):
        _, _, table, _, lhs, acc, chosen, spec, wide = self.args
        transform(lhs, table, acc)
        outgoing(acc, chosen, spec, wide, out)


FILTER_SCRATCH = [
    pltpu.VMEM((ROWS, FFT_LEN), jnp.bfloat16),
    pltpu.VMEM((4, ROWS, LANES), jnp.float32),
    pltpu.VMEM((CAP, LANES, BAND), jnp.bfloat16),
    pltpu.VMEM((2, ROWS // 2, BAND), jnp.bfloat16),
    pltpu.VMEM((LANES * 6, LANES), jnp.float32),
]


HALF = 512
TOTAL = 1024
TIMES = 2 * NSPEC
LINES = TOTAL * 3 // 2


def build_places(map_ref, places):
    row = lax.broadcasted_iota(jnp.int32, (LANES, LANES), 0)
    lane = lax.broadcasted_iota(jnp.int32, (LANES, LANES), 1)
    listed = jnp.zeros((LANES, LANES), jnp.float32)
    for x in range(4):
        stations = jnp.broadcast_to(map_ref[x : x + 1, :], (LANES, LANES)).astype(jnp.float32)
        listed = jnp.where(((row >> 4) & 3) == x, stations, listed)
    first = (row >> 6) * 64 + (row & 15) * 4
    want = lax.broadcasted_iota(jnp.int32, (LANES, TOTAL), 1)
    for pair in range(4):
        station = jnp.sum(jnp.where(lane == first + pair, listed, 0.0), axis=1, keepdims=True)
        for p in range(2):
            a = 2 * pair + p
            target = 2 * station.astype(jnp.int32) + p
            places[a * LANES : (a + 1) * LANES, :] = jnp.where(want == target, 1.0, 0.0).astype(jnp.bfloat16)


def order_rows(part, got, places, gathered, lines, columns):
    gathered[...] = got.reshape(LINES, LANES)[...].astype(jnp.float32)
    spots = [(k, p, b) for k in range(CAP) for p in range(2) for b in range(2)]
    for i, (k, p, b) in enumerate(spots):
        base = 2 * k + p
        first = gathered[pl.ds(base + b * 384, 64, stride=6), :]
        second = gathered[pl.ds(base + (b + 2) * 384, 64, stride=6), :]
        block = jnp.concatenate([first, second], axis=0).T.astype(jnp.bfloat16)
        for a in range(STREAMS):
            lines[i * SPAN : (i + 1) * SPAN, a * LANES : (a + 1) * LANES] = block[a * SPAN : (a + 1) * SPAN]
    ordered = jnp.dot(lines[...], places[...], preferred_element_type=jnp.float32)
    for i, (k, p, b) in enumerate(spots):
        row = p * TIMES + b * NSPEC + part * SPAN
        columns[k, row : row + SPAN, :] = ordered[i * SPAN : (i + 1) * SPAN].astype(jnp.bfloat16)


def filter_and_turn(
    frames, tap_ref, table_ref, count_ref, map_ref, columns, lhs, acc, chosen, spec, wide, table, places, gathered,
    lines, got, sent, stage, other, table_sem, send_z, recv_z, send_x, recv_x, send_y, recv_y, local_sems
):
    stn = lax.axis_index("stn")
    blk = lax.axis_index("blk")
    g = lax.rem(stn, 16)
    h = lax.div(stn, 16)
    x = lax.div(h, 2)
    y_hi = lax.rem(h, 2)
    y = 2 * y_hi + blk

    def at(x_to, y_hi_to, g_to):
        return (x_to * 2 + y_hi_to) * 16 + g_to

    near = {"stn": stn, "blk": 1 - blk}
    cross = {"stn": at(x, 1 - y_hi, g), "blk": 1 - blk}
    ring_z = [{"stn": at(x, y_hi, lax.rem(g + j, 16)), "blk": blk} for j in range(1, 16)]
    ring_x = [{"stn": at(lax.rem(x + j, 4), y_hi, g), "blk": blk} for j in range(1, 4)]

    barrier = pltpu.get_barrier_semaphore()
    partners = [*ring_z, *ring_x, near, cross]
    for partner in partners:
        pl.semaphore_signal(barrier, inc=1, device_id=partner, device_id_type=MESH)
    load_table = pltpu.make_async_copy(table_ref.at[pl.ds(0, FFT_LEN)], table, table_sem.at[0])
    load_table.start()
    bank = Filter(frames, tap_ref, table, count_ref, lhs, acc, chosen, spec, wide)

    def remote(src, dst, send, recv, device):
        copy = pltpu.make_async_remote_copy(
            src_ref=src, dst_ref=dst, send_sem=send, recv_sem=recv, device_id=device, device_id_type=MESH
        )
        copy.start()

    def drain(ref, sem):
        pltpu.make_async_copy(ref, ref, sem).wait()

    def own_z(c):
        return pltpu.make_async_copy(sent.at[c, g], stage.at[c, g], local_sems.at[0, c])

    def own_x(c, half):
        if half == 0:
            return pltpu.make_async_copy(
                stage.at[c, :, x * 2 + y_hi], got.at[c, y, x], local_sems.at[1, c]
            )
        return pltpu.make_async_copy(
            stage.at[c, :, x * 2 + 1 - y_hi], other.at[c, x], local_sems.at[2, c]
        )

    def go_z(c):
        own_z(c).start()
        for j in (8, 7, 9, 6, 10, 5, 11, 4, 12, 3, 13, 2, 14, 1, 15):
            remote(
                sent.at[c, lax.rem(g + j, 16)], stage.at[c, g], send_z.at[c], recv_z.at[c], ring_z[j - 1]
            )

    def go_x(c):
        own_z(c).wait()
        drain(stage.at[c, pl.ds(0, 15)], recv_z.at[c])
        own_x(c, 0).start()
        own_x(c, 1).start()
        for j in range(1, 4):
            x_to = lax.rem(x + j, 4)
            remote(
                stage.at[c, :, x_to * 2 + 1 - y_hi], other.at[c, x], send_x.at[1, c], recv_x.at[1, c], ring_x[j - 1]
            )
        for j in range(1, 4):
            x_to = lax.rem(x + j, 4)
            remote(
                stage.at[c, :, x_to * 2 + y_hi], got.at[c, y, x], send_x.at[0, c], recv_x.at[0, c], ring_x[j - 1]
            )

    def go_y(c):
        own_x(c, 1).wait()
        drain(other.at[c, pl.ds(0, 3)], recv_x.at[1, c])
        remote(other.at[c], got.at[c, y], send_y.at[0, c], recv_y.at[0, c], cross)
        own_x(c, 0).wait()
        drain(other.at[c, pl.ds(0, 3)], recv_x.at[0, c])
        remote(got.at[c, y], got.at[c, y], send_y.at[1, c], recv_y.at[1, c], near)

    def go_forward(c):
        drain(other.at[c], recv_y.at[0, c])
        remote(got.at[c, 3 - y], got.at[c, 3 - y], send_y.at[2, c], recv_y.at[2, c], near)

    def order(c):
        drain(other.at[c], recv_y.at[1, c])
        drain(other.at[c], recv_y.at[2, c])
        order_rows(c, got.at[c], places, gathered, lines, columns)

    bank.start()
    bank.fold(0, 0)
    bank.fold(0, 1)
    load_table.wait()
    bank.finish(sent.at[0])
    pl.semaphore_wait(barrier, len(partners))
    go_z(0)
    bank.fold(1, 0)
    bank.fold(1, 1)
    bank.finish(sent.at[1])
    go_z(1)
    bank.fold(2, 0)
    go_x(0)
    bank.fold(2, 1)
    bank.finish(sent.at[2])
    go_z(2)
    go_y(0)
    build_places(map_ref, places)
    go_x(1)
    go_forward(0)
    go_y(1)
    go_x(2)
    go_forward(1)
    go_y(2)
    go_forward(2)
    for c in range(PARTS):
        order(c)
    for c in range(PARTS):
        drain(stage.at[c, pl.ds(0, 15)], send_z.at[c])
        for k in range(2):
            drain(other.at[c, pl.ds(0, 3)], send_x.at[k, c])
        for k in range(3):
            drain(other.at[c], send_y.at[k, c])


def run_filter_and_turn(voltages, station_map, chan_counts):
    vmem = pl.BlockSpec(memory_space=pltpu.VMEM)
    dma = pltpu.SemaphoreType.DMA
    ratios, table = tables_of()
    padded = np.pad(table, ((0, 3 * FFT_LEN), (0, 0)))
    return pl.pallas_call(
        filter_and_turn,
        out_shape=jax.ShapeDtypeStruct((CAP, 2 * TIMES, TOTAL), jnp.bfloat16),
        in_specs=[vmem, vmem, pl.BlockSpec(memory_space=pl.ANY), vmem, vmem],
        out_specs=vmem,
        scratch_shapes=[
            *FILTER_SCRATCH,
            pltpu.VMEM((FFT_LEN, 2 * BAND), jnp.bfloat16),
            pltpu.VMEM((TOTAL, TOTAL), jnp.bfloat16),
            pltpu.VMEM((LINES, LANES), jnp.float32),
            pltpu.VMEM((12 * SPAN, TOTAL), jnp.bfloat16),
            pltpu.VMEM((PARTS, 4, 4, 16, CAP, 2, LANES), jnp.bfloat16),
            pltpu.VMEM((PARTS, 16, 8, CAP, 2, LANES), jnp.bfloat16),
            pltpu.VMEM((PARTS, 16, 8, CAP, 2, LANES), jnp.bfloat16),
            pltpu.VMEM((PARTS, 4, 16, CAP, 2, LANES), jnp.bfloat16),
            dma((1,)),
            dma((PARTS,)),
            dma((PARTS,)),
            dma((2, PARTS)),
            dma((2, PARTS)),
            dma((3, PARTS)),
            dma((3, PARTS)),
            dma((3, PARTS)),
        ],
        compiler_params=pltpu.CompilerParams(
            collective_id=0, has_side_effects=True, vmem_limit_bytes=36 * 1024 * 1024
        ),
        name="filter_and_turn",
    )(
        run_bring_in(voltages),
        jnp.asarray(ratios),
        jnp.asarray(padded),
        chan_counts.reshape(1, LANES),
        station_map.reshape(4, LANES),
    )


COLUMNS = 512


def correlate(columns, count_ref, out_ref, left):
    k = pl.program_id(0)
    part = pl.program_id(1)

    @pl.when(part == 0)
    def _():
        start = pl.multiple_of(lax.axis_index("blk") * HALF, HALF)
        mine = columns[k, :, pl.ds(start, HALF)]
        left[...] = mine.T

    me = lax.axis_index("stn")
    lane = lax.broadcasted_iota(jnp.int32, (1, LANES), 1)
    live = jnp.sum(jnp.where(lane == me, count_ref[...], 0).astype(jnp.float32), axis=1, keepdims=True)
    scale = jnp.where(k.astype(jnp.float32) < live, 1.0 / TIMES, 0.0)
    for n in range(COLUMNS // 256):
        right = columns[k, :, pl.ds(pl.multiple_of(part * COLUMNS + n * 256, 256), 256)]
        turned = jnp.concatenate([-right[TIMES:], right[:TIMES]], axis=0)
        for i, other in enumerate((right, turned)):
            product = jnp.dot(left[...], other, preferred_element_type=jnp.float32)
            out_ref[0, 0, i, :, n * 256 : (n + 1) * 256] = (product * scale).astype(jnp.bfloat16)


def run_correlate(columns, chan_counts):
    return pl.pallas_call(
        correlate,
        grid=(CAP, TOTAL // COLUMNS),
        out_shape=jax.ShapeDtypeStruct((1, CAP, 2, HALF, TOTAL), jnp.bfloat16),
        in_specs=[
            pl.BlockSpec(memory_space=pltpu.VMEM),
            pl.BlockSpec(memory_space=pltpu.VMEM),
        ],
        out_specs=pl.BlockSpec((1, 1, 2, HALF, COLUMNS), lambda k, i: (0, k, 0, 0, i)),
        scratch_shapes=[pltpu.VMEM((HALF, 2 * TIMES), jnp.bfloat16)],
        compiler_params=pltpu.CompilerParams(vmem_limit_bytes=32 * 1024 * 1024),
        name="correlate",
    )(columns, chan_counts.reshape(1, LANES))


def body(voltages, station_map, chan_counts):
    columns = run_filter_and_turn(voltages, station_map, chan_counts)
    return run_correlate(columns, chan_counts)


def solution(mesh):
    return jax.shard_map(
        body,
        mesh=mesh,
        in_specs=(P("stn", "blk", None, None, None), P(), P()),
        out_specs=P("stn", None, None, "blk", None),
        check_vma=False,
    )
```

```python
import functools
import math

import jax
import jax.numpy as jnp
import ml_dtypes
import numpy as np
from jax import lax
from jax.experimental import pallas as pl
from jax.experimental.pallas import tpu as pltpu
from jax.sharding import PartitionSpec as P

FFT_LEN = 4096
TAPS = 16
CAP = 3
NSPEC = 48
FRAMES = 63
STREAMS = 8
BAND = 256
LANES = 128
TILES = FFT_LEN // LANES
PARTS = 3
SPAN = NSPEC // PARTS
BLOCK = 16
ROWS = SPAN * STREAMS * 2
LAST = TAPS // 2
OUTER = sorted((t for t in range(TAPS) if t not in (LAST - 1, LAST)), key=lambda t: -abs(t - 7.5))
MESH = pl.DeviceIdType.MESH


def prototype():
    points = np.arange(TAPS * FFT_LEN) + 0.5
    span_len = TAPS * FFT_LEN
    filt = np.sinc((points - span_len / 2) / FFT_LEN) * (
        0.5 - 0.5 * np.cos(2.0 * math.pi * points / span_len)
    )
    filt = filt / np.sqrt(np.sum(filt * filt))
    return filt.reshape(TAPS, FFT_LEN)


def tables_of():
    filt = prototype()
    positions = np.arange(FFT_LEN)
    pivot = np.where(positions < FFT_LEN // 2, filt[LAST], filt[LAST - 1])
    ratios = (filt / pivot).reshape(TAPS, TILES, LANES).transpose(1, 0, 2)
    phase = (positions[:, None] * np.arange(BAND)[None, :] % FFT_LEN) * (2.0 * math.pi / FFT_LEN)
    table = np.concatenate([np.cos(phase), np.sin(phase)], axis=1) * pivot[:, None]
    return np.ascontiguousarray(ratios.astype(np.float32)), table.astype(ml_dtypes.bfloat16)


def fold_tile(tap_ref, frames, part, half, tile, lhs):
    pivot, partner = (LAST, LAST - 1) if half == 0 else (LAST - 1, LAST)
    taps = tap_ref[tile]
    low = {
        t: jnp.broadcast_to(taps[t : t + 1], (16, LANES)).astype(jnp.bfloat16)
        for t in [*OUTER, partner]
    }
    lanes = pl.ds(pl.multiple_of(tile * LANES, LANES), LANES)
    for base in range(0, SPAN, BLOCK):
        first = part * SPAN + base
        volts = [frames[first + r, tile] for r in range(BLOCK + TAPS - 1)]
        for s in range(BLOCK):
            small = low[OUTER[0]] * volts[s + OUTER[0]]
            for t in [*OUTER[1:], partner]:
                small = small + low[t] * volts[s + t]
            row = (base + s) * 16
            lhs[row : row + 16, lanes] = volts[s + pivot] + small


def choose_slots(count_ref, chosen):
    row = lax.broadcasted_iota(jnp.int32, (LANES, LANES), 0)
    device = (row & 7) * 16 + (row >> 3)
    lane = lax.broadcasted_iota(jnp.int32, (LANES, LANES), 1)
    counts = jnp.broadcast_to(count_ref[...], (LANES, LANES)).astype(jnp.float32)
    offset = jnp.sum(jnp.where(lane < device, counts, 0.0), axis=1, keepdims=True)
    count = jnp.sum(jnp.where(lane == device, counts, 0.0), axis=1, keepdims=True)
    band = lax.broadcasted_iota(jnp.int32, (LANES, BAND), 1)
    for k in range(CAP):
        pick = (offset + jnp.minimum(float(k), count - 1.0)).astype(jnp.int32)
        chosen[k] = jnp.where(band == pick, 1.0, 0.0).astype(jnp.bfloat16)


def transform(lhs, table, acc):
    got = jnp.dot(lhs[...], table[...], preferred_element_type=jnp.float32)
    for q in range(4):
        acc[q] = got[:, q * LANES : (q + 1) * LANES]


def outgoing(acc, chosen, spec, wide, out):
    for a in range(STREAMS):
        part = {}
        for p in range(2):
            for q in range(4):
                part[p, q] = acc[q, pl.ds(2 * a + p, SPAN, stride=16), :]
        for q in range(2):
            cols = slice(q * LANES, (q + 1) * LANES)
            rows = slice(a * SPAN, (a + 1) * SPAN)
            spec[0, rows, cols] = (part[0, q] + part[1, q + 2]).astype(jnp.bfloat16)
            spec[1, rows, cols] = (part[1, q] - part[0, q + 2]).astype(jnp.bfloat16)
    for k in range(CAP):
        for p in range(2):
            turned = lax.dot_general(
                chosen[k], spec[p], (((1,), (1,)), ((), ())), preferred_element_type=jnp.float32
            )
            wide[pl.ds(2 * k + p, LANES, stride=6), :] = turned
    out.reshape(LANES * 6, LANES)[...] = wide[...].astype(jnp.bfloat16)


def bring_in(volt_ref, out_ref, sems):
    copies = [
        pltpu.make_async_copy(volt_ref.at[a], out_ref.at[:, :, a], sems.at[a]) for a in range(STREAMS)
    ]
    for copy in copies:
        copy.start()
    for copy in copies:
        copy.wait()


def run_bring_in(voltages):
    tiles = voltages.reshape(STREAMS, FRAMES, 2, TILES, LANES).transpose(0, 1, 3, 2, 4)
    frames = pl.pallas_call(
        bring_in,
        out_shape=jax.ShapeDtypeStruct((FRAMES, TILES, STREAMS, 2, LANES), jnp.bfloat16),
        in_specs=[pl.BlockSpec(memory_space=pl.ANY)],
        out_specs=pl.BlockSpec(memory_space=pltpu.VMEM),
        scratch_shapes=[pltpu.SemaphoreType.DMA((STREAMS,))],
        compiler_params=pltpu.CompilerParams(vmem_limit_bytes=42 * 1024 * 1024),
        name="bring_in",
    )(tiles)
    return frames.reshape(FRAMES, TILES, 16, LANES)


class Filter:
    def __init__(self, frames, tap_ref, table, count_ref, lhs, acc, chosen, spec, wide):
        self.args = frames, tap_ref, table, count_ref, lhs, acc, chosen, spec, wide

    def start(self):
        choose_slots(self.args[3], self.args[6])

    def fold(self, part, half):
        frames, tap_ref, lhs = self.args[0], self.args[1], self.args[4]

        def step(i, carry):
            for u in range(2):
                fold_tile(tap_ref, frames, part, half, half * (TILES // 2) + 2 * i + u, lhs)
            return carry

        lax.fori_loop(0, TILES // 4, step, 0)

    def finish(self, out):
        _, _, table, _, lhs, acc, chosen, spec, wide = self.args
        transform(lhs, table, acc)
        outgoing(acc, chosen, spec, wide, out)


FILTER_SCRATCH = [
    pltpu.VMEM((ROWS, FFT_LEN), jnp.bfloat16),
    pltpu.VMEM((4, ROWS, LANES), jnp.float32),
    pltpu.VMEM((CAP, LANES, BAND), jnp.bfloat16),
    pltpu.VMEM((2, ROWS // 2, BAND), jnp.bfloat16),
    pltpu.VMEM((LANES * 6, LANES), jnp.float32),
]


HALF = 512
TOTAL = 1024
TIMES = 2 * NSPEC
LINES = TOTAL * 3 // 2


def build_places(map_ref, places):
    row = lax.broadcasted_iota(jnp.int32, (LANES, LANES), 0)
    lane = lax.broadcasted_iota(jnp.int32, (LANES, LANES), 1)
    listed = jnp.zeros((LANES, LANES), jnp.float32)
    for x in range(4):
        stations = jnp.broadcast_to(map_ref[x : x + 1, :], (LANES, LANES)).astype(jnp.float32)
        listed = jnp.where(((row >> 4) & 3) == x, stations, listed)
    first = (row >> 6) * 64 + (row & 15) * 4
    want = lax.broadcasted_iota(jnp.int32, (LANES, TOTAL), 1)
    for pair in range(4):
        station = jnp.sum(jnp.where(lane == first + pair, listed, 0.0), axis=1, keepdims=True)
        for p in range(2):
            a = 2 * pair + p
            target = 2 * station.astype(jnp.int32) + p
            places[a * LANES : (a + 1) * LANES, :] = jnp.where(want == target, 1.0, 0.0).astype(jnp.bfloat16)


def order_rows(part, got, places, gathered, lines, columns):
    gathered[...] = got.reshape(LINES, LANES)[...].astype(jnp.float32)
    spots = [(k, p, b) for k in range(CAP) for p in range(2) for b in range(2)]
    for i, (k, p, b) in enumerate(spots):
        base = 2 * k + p
        first = gathered[pl.ds(base + b * 384, 64, stride=6), :]
        second = gathered[pl.ds(base + (b + 2) * 384, 64, stride=6), :]
        block = jnp.concatenate([first, second], axis=0).T.astype(jnp.bfloat16)
        for a in range(STREAMS):
            lines[i * SPAN : (i + 1) * SPAN, a * LANES : (a + 1) * LANES] = block[a * SPAN : (a + 1) * SPAN]
    ordered = jnp.dot(lines[...], places[...], preferred_element_type=jnp.float32)
    for i, (k, p, b) in enumerate(spots):
        row = p * TIMES + b * NSPEC + part * SPAN
        columns[k, row : row + SPAN, :] = ordered[i * SPAN : (i + 1) * SPAN].astype(jnp.bfloat16)


def filter_and_turn(
    frames, tap_ref, table_ref, count_ref, map_ref, columns, lhs, acc, chosen, spec, wide, table, places, gathered,
    lines, got, sent, stage, other, table_sem, send_z, recv_z, send_x, recv_x, send_y, recv_y, local_sems
):
    stn = lax.axis_index("stn")
    blk = lax.axis_index("blk")
    g = lax.rem(stn, 16)
    h = lax.div(stn, 16)
    x = lax.div(h, 2)
    y_hi = lax.rem(h, 2)
    y = 2 * y_hi + blk

    def at(x_to, y_hi_to, g_to):
        return (x_to * 2 + y_hi_to) * 16 + g_to

    near = {"stn": stn, "blk": 1 - blk}
    cross = {"stn": at(x, 1 - y_hi, g), "blk": 1 - blk}
    ring_z = [{"stn": at(x, y_hi, lax.rem(g + j, 16)), "blk": blk} for j in range(1, 16)]
    ring_x = [{"stn": at(lax.rem(x + j, 4), y_hi, g), "blk": blk} for j in range(1, 4)]

    barrier = pltpu.get_barrier_semaphore()
    partners = [*ring_z, *ring_x, near, cross]
    for partner in partners:
        pl.semaphore_signal(barrier, inc=1, device_id=partner, device_id_type=MESH)
    load_table = pltpu.make_async_copy(table_ref.at[pl.ds(0, FFT_LEN)], table, table_sem.at[0])
    load_table.start()
    bank = Filter(frames, tap_ref, table, count_ref, lhs, acc, chosen, spec, wide)

    def remote(src, dst, send, recv, device):
        copy = pltpu.make_async_remote_copy(
            src_ref=src, dst_ref=dst, send_sem=send, recv_sem=recv, device_id=device, device_id_type=MESH
        )
        copy.start()

    def drain(ref, sem):
        pltpu.make_async_copy(ref, ref, sem).wait()

    def own_z(c):
        return pltpu.make_async_copy(sent.at[c, g], stage.at[c, g], local_sems.at[0, c])

    def own_x(c, half):
        if half == 0:
            return pltpu.make_async_copy(
                stage.at[c, :, x * 2 + y_hi], got.at[c, y, x], local_sems.at[1, c]
            )
        return pltpu.make_async_copy(
            stage.at[c, :, x * 2 + 1 - y_hi], other.at[c, x], local_sems.at[2, c]
        )

    def go_z(c):
        own_z(c).start()
        for j in (8, 7, 9, 6, 10, 5, 11, 4, 12, 3, 13, 2, 14, 1, 15):
            remote(
                sent.at[c, lax.rem(g + j, 16)], stage.at[c, g], send_z.at[c], recv_z.at[c], ring_z[j - 1]
            )

    def go_x(c):
        own_z(c).wait()
        drain(stage.at[c, pl.ds(0, 15)], recv_z.at[c])
        own_x(c, 0).start()
        own_x(c, 1).start()
        for j in (2, 1, 3):
            x_to = lax.rem(x + j, 4)
            remote(
                stage.at[c, :, x_to * 2 + 1 - y_hi], other.at[c, x], send_x.at[1, c], recv_x.at[1, c], ring_x[j - 1]
            )
        for j in (2, 1, 3):
            x_to = lax.rem(x + j, 4)
            remote(
                stage.at[c, :, x_to * 2 + y_hi], got.at[c, y, x], send_x.at[0, c], recv_x.at[0, c], ring_x[j - 1]
            )

    def go_y(c):
        own_x(c, 1).wait()
        drain(other.at[c, pl.ds(0, 3)], recv_x.at[1, c])
        remote(other.at[c], got.at[c, y], send_y.at[0, c], recv_y.at[0, c], cross)
        own_x(c, 0).wait()
        drain(other.at[c, pl.ds(0, 3)], recv_x.at[0, c])
        remote(got.at[c, y], got.at[c, y], send_y.at[1, c], recv_y.at[1, c], near)

    def go_forward(c):
        drain(other.at[c], recv_y.at[0, c])
        remote(got.at[c, 3 - y], got.at[c, 3 - y], send_y.at[2, c], recv_y.at[2, c], near)

    def order(c):
        drain(other.at[c], recv_y.at[1, c])
        drain(other.at[c], recv_y.at[2, c])
        order_rows(c, got.at[c], places, gathered, lines, columns)

    bank.start()
    bank.fold(0, 0)
    bank.fold(0, 1)
    load_table.wait()
    bank.finish(sent.at[0])
    pl.semaphore_wait(barrier, len(partners))
    go_z(0)
    bank.fold(1, 0)
    bank.fold(1, 1)
    bank.finish(sent.at[1])
    go_z(1)
    bank.fold(2, 0)
    go_x(0)
    bank.fold(2, 1)
    bank.finish(sent.at[2])
    go_z(2)
    go_y(0)
    go_x(1)
    build_places(map_ref, places)
    go_forward(0)
    go_y(1)
    go_x(2)
    go_forward(1)
    go_y(2)
    go_forward(2)
    for c in range(PARTS):
        order(c)
    for c in range(PARTS):
        drain(stage.at[c, pl.ds(0, 15)], send_z.at[c])
        for k in range(2):
            drain(other.at[c, pl.ds(0, 3)], send_x.at[k, c])
        for k in range(3):
            drain(other.at[c], send_y.at[k, c])


def run_filter_and_turn(voltages, station_map, chan_counts):
    vmem = pl.BlockSpec(memory_space=pltpu.VMEM)
    dma = pltpu.SemaphoreType.DMA
    ratios, table = tables_of()
    padded = np.pad(table, ((0, 3 * FFT_LEN), (0, 0)))
    return pl.pallas_call(
        filter_and_turn,
        out_shape=jax.ShapeDtypeStruct((CAP, 2 * TIMES, TOTAL), jnp.bfloat16),
        in_specs=[vmem, vmem, pl.BlockSpec(memory_space=pl.ANY), vmem, vmem],
        out_specs=vmem,
        scratch_shapes=[
            *FILTER_SCRATCH,
            pltpu.VMEM((FFT_LEN, 2 * BAND), jnp.bfloat16),
            pltpu.VMEM((TOTAL, TOTAL), jnp.bfloat16),
            pltpu.VMEM((LINES, LANES), jnp.float32),
            pltpu.VMEM((12 * SPAN, TOTAL), jnp.bfloat16),
            pltpu.VMEM((PARTS, 4, 4, 16, CAP, 2, LANES), jnp.bfloat16),
            pltpu.VMEM((PARTS, 16, 8, CAP, 2, LANES), jnp.bfloat16),
            pltpu.VMEM((PARTS, 16, 8, CAP, 2, LANES), jnp.bfloat16),
            pltpu.VMEM((PARTS, 4, 16, CAP, 2, LANES), jnp.bfloat16),
            dma((1,)),
            dma((PARTS,)),
            dma((PARTS,)),
            dma((2, PARTS)),
            dma((2, PARTS)),
            dma((3, PARTS)),
            dma((3, PARTS)),
            dma((3, PARTS)),
        ],
        compiler_params=pltpu.CompilerParams(
            collective_id=0, has_side_effects=True, vmem_limit_bytes=36 * 1024 * 1024
        ),
        name="filter_and_turn",
    )(
        run_bring_in(voltages),
        jnp.asarray(ratios),
        jnp.asarray(padded),
        chan_counts.reshape(1, LANES),
        station_map.reshape(4, LANES),
    )


COLUMNS = 512


def correlate(columns, count_ref, out_ref, left):
    k = pl.program_id(0)
    part = pl.program_id(1)

    @pl.when(part == 0)
    def _():
        start = pl.multiple_of(lax.axis_index("blk") * HALF, HALF)
        mine = columns[k, :, pl.ds(start, HALF)]
        left[...] = mine.T

    me = lax.axis_index("stn")
    lane = lax.broadcasted_iota(jnp.int32, (1, LANES), 1)
    live = jnp.sum(jnp.where(lane == me, count_ref[...], 0).astype(jnp.float32), axis=1, keepdims=True)
    scale = jnp.where(k.astype(jnp.float32) < live, 1.0 / TIMES, 0.0)
    for n in range(COLUMNS // 256):
        right = columns[k, :, pl.ds(pl.multiple_of(part * COLUMNS + n * 256, 256), 256)]
        turned = jnp.concatenate([-right[TIMES:], right[:TIMES]], axis=0)
        for i, other in enumerate((right, turned)):
            product = jnp.dot(left[...], other, preferred_element_type=jnp.float32)
            out_ref[0, 0, i, :, n * 256 : (n + 1) * 256] = (product * scale).astype(jnp.bfloat16)


def run_correlate(columns, chan_counts):
    return pl.pallas_call(
        correlate,
        grid=(CAP, TOTAL // COLUMNS),
        out_shape=jax.ShapeDtypeStruct((1, CAP, 2, HALF, TOTAL), jnp.bfloat16),
        in_specs=[
            pl.BlockSpec(memory_space=pltpu.VMEM),
            pl.BlockSpec(memory_space=pltpu.VMEM),
        ],
        out_specs=pl.BlockSpec((1, 1, 2, HALF, COLUMNS), lambda k, i: (0, k, 0, 0, i)),
        scratch_shapes=[pltpu.VMEM((HALF, 2 * TIMES), jnp.bfloat16)],
        compiler_params=pltpu.CompilerParams(vmem_limit_bytes=32 * 1024 * 1024),
        name="correlate",
    )(columns, chan_counts.reshape(1, LANES))


def body(voltages, station_map, chan_counts):
    columns = run_filter_and_turn(voltages, station_map, chan_counts)
    return run_correlate(columns, chan_counts)


def solution(mesh):
    return jax.shard_map(
        body,
        mesh=mesh,
        in_specs=(P("stn", "blk", None, None, None), P(), P()),
        out_specs=P("stn", None, None, "blk", None),
        check_vma=False,
    )
```
